256 devices in a mesh: ctx: 16 (over y_hi, x, core), exp: 8 (over z), dp: 2 (over y_lo).
Axes of the slice: x: 4, y: 4 (y_hi: 2, y_lo: 2; y = y_hi * 2 + y_lo), z: 8, core: 2. Of those that a mesh axis runs over, the one named last changes fastest.
Arguments:
- tokens: bfloat16 [2, 2048, 4096], P('dp', 'ctx'), may hold values from -6 to 6
- norm_in: bfloat16 [4096], replicated, may hold values from 0.099609375 to 1.8984375
- w_qkv: bfloat16 [4096, 8, 6, 128], P('dp', 'exp')
- w_out: bfloat16 [8, 4, 128, 4096], P('exp', None, None, 'dp'), may hold values from -0.375 to 0.375
- norm_mid: bfloat16 [4096], replicated, may hold values from 0.099609375 to 1.8984375
- w_router: bfloat16 [4096, 8], replicated, may hold values from -0.09375 to 0.09375
- w_gate_up: bfloat16 [8, 4096, 2, 8192], P('exp', 'dp', None, 'ctx'), may hold values from -0.09375 to 0.09375
- w_down: bfloat16 [8, 8192, 4096], P('exp', 'ctx', 'dp'), may hold values from -0.0625 to 0.0625
- expert_ids: int32 [2, 2048, 2], P('dp', ('ctx', 'exp')), may hold values from 0 to 7, as said below
- slot_index: int32 [2, 2048, 2], P('dp', ('ctx', 'exp')), may hold values from 0 to 5, as said below
Outputs:
- layer_out: bfloat16 [2, 2048, 4096], P('dp', ('ctx', 'exp'))
The draws below stay inside these ranges and needn't reach their ends.
Inputs may be any that keep to these rules, and one draw needn't show every extreme that they name: `expert_ids`: each token names two different experts; in every aligned block of 16 tokens (the tokens of one device) the numbers of choices of the experts are, in some order, 6, 5, 4, 4, 4, 3, 3 and 3, so that no expert is named more than 6 times and one exactly 6 times. `slot_index`: a choice's slot is the number of earlier choices of the same expert in its block of 16 tokens, a token's first choice counting before its second.
All inputs are finite; a program needn't handle non-finite values.
Results may differ from the reference program's by a relative error of at most 0.022.
The reference program's roundings to bfloat16 on the way count: a program that leaves them out, or rounds other values in their place, can miss the bound.
Values may be sent and summed in bfloat16 or wider, within the bound.
No kernel may reach another device: no remote copies, remote signals or barrier semaphores. Data moves between devices by JAX's collectives and lax.ppermute only.
A program may use at most 128 MiB of HBM per device.

```python
import math
import jax
import jax.numpy as jnp
import numpy as np
from jax import lax

D = 4096
HEADS = 32
KV_HEADS = 8
HEAD_SIZE = 128
EXPERTS = 8
FF_WIN = 8192
LEN = 2048
GROUP = 4
MOE_ROWS = 16
CAP = 6
FF_DEV = 512
N_DP = 2


PAIR_TABLE = np.array([[0, 1], [0, 2], [0, 3], [0, 4], [0, 5], [0, 6], [1, 2], [1, 3], [1, 7], [1, 5], [2, 4], [2, 6], [3, 4], [3, 7], [4, 5], [6, 7]], dtype=np.int32)


def routing_table(key):
    key = jax.random.fold_in(key, 7)
    blocks = N_DP * LEN // MOE_ROWS
    unit_count = MOE_ROWS // 16
    key_labels, key_orders, key_flips = jax.random.split(key, 3)
    labels = jax.vmap(lambda subkey: jax.random.permutation(subkey, EXPERTS))(jax.random.split(key_labels, blocks))
    orders = jax.vmap(lambda subkey: jax.random.permutation(subkey, 16))(jax.random.split(key_orders, blocks * unit_count))
    orders = orders.reshape(blocks, unit_count, 16)
    template = jnp.asarray(PAIR_TABLE)
    picked = template[orders]
    flipped = jax.random.randint(key_flips, (blocks, unit_count, 16, 1), 0, 2)
    picked = jnp.where(flipped == 1, picked[..., ::-1], picked)
    choice_ids = jnp.take_along_axis(labels, picked.reshape(blocks, MOE_ROWS * 2), axis=1).astype(jnp.int32)
    matches = choice_ids[:, :, None] == choice_ids[:, None, :]
    positions = jnp.arange(MOE_ROWS * 2)
    earlier = positions[None, :] < positions[:, None]
    slot_ids = jnp.sum(jnp.where(jnp.logical_and(matches, earlier[None]), 1, 0), axis=2).astype(jnp.int32)
    return (choice_ids.reshape(N_DP, LEN, 2), slot_ids.reshape(N_DP, LEN, 2))


def draw_expert_ids(key, part):
    return routing_table(key)[0]


def draw_slot_index(key, part):
    return routing_table(key)[1]


def draw_w_qkv(key, part):
    key = jax.random.fold_in(key, 11)
    key_base = jax.random.fold_in(key, 0)
    base = jax.random.normal(key_base, (D, KV_HEADS, GROUP + 2, HEAD_SIZE), jnp.float32)
    scales = jnp.where(jnp.arange(GROUP + 2) < GROUP, 2.0, 1.0) * D ** (-0.5)
    weights = base * scales[None, None, :, None]
    return weights.astype(jnp.bfloat16)


def levels(key, extent, shards, least, top_value):
    def one(axis_at, blocks):
        heights = jax.random.uniform(jax.random.fold_in(jax.random.fold_in(key, 6), axis_at), (blocks,), jnp.float32, least / len(shards), top_value / len(shards))
        return jnp.repeat(jnp.exp(heights), extent[axis_at] // blocks).reshape((-1,) + (1,) * (len(extent) - axis_at - 1))

    factor_of = one(*shards[0])
    for cut in shards[1:]:
        factor_of = factor_of * one(*cut)
    return factor_of


def gaussian(stream_key, dims, deviation, most, cuts=(), kind=jnp.bfloat16):
    values = jax.random.normal(stream_key, dims, jnp.float32) * deviation
    if len(cuts) > 0:
        values = levels(stream_key, dims, cuts, -0.22, 0.18) * values
    return jnp.clip(values, min=-most, max=most).astype(kind)


def setup_inputs(seed: int = 0) -> dict:
    seeds = jax.random.split(jax.random.key(seed), 11)
    tokens = gaussian(seeds[0], (N_DP, LEN, D), 1.0, 6.0, ((0, 2), (1, 16)))
    norm_in = jnp.clip(1.0 + 0.18 * jax.random.normal(seeds[1], (D,), jnp.float32), 0.099609375, 1.8984375).astype(jnp.bfloat16)
    w_qkv = draw_w_qkv(jax.random.fold_in(seeds[10], 71), 0)
    w_out = gaussian(seeds[3], (KV_HEADS, GROUP, HEAD_SIZE, D), (2 * HEAD_SIZE) ** -0.5, 0.375, ((0, 8), (3, 2)))
    norm_mid = jnp.clip(1.0 + 0.18 * jax.random.normal(seeds[4], (D,), jnp.float32), 0.099609375, 1.8984375).astype(jnp.bfloat16)
    w_router = gaussian(seeds[5], (D, EXPERTS), D ** -0.5, 0.09375)
    w_gate_up = gaussian(seeds[6], (EXPERTS, D, 2, FF_WIN), D ** -0.5, 0.09375, ((0, 8), (1, 2), (3, 16)))
    w_down = gaussian(seeds[7], (EXPERTS, FF_WIN, D), FF_WIN ** -0.5, 0.0625, ((0, 8), (1, 16), (2, 2)))
    expert_ids = draw_expert_ids(jax.random.fold_in(seeds[10], 71), 0)
    slot_index = draw_slot_index(jax.random.fold_in(seeds[10], 71), 0)
    return {"tokens": tokens, "norm_in": norm_in, "w_qkv": w_qkv, "w_out": w_out, "norm_mid": norm_mid, "w_router": w_router, "w_gate_up": w_gate_up, "w_down": w_down, "expert_ids": expert_ids, "slot_index": slot_index}


EPSILON = 1e-05
ROPE_BASE = 1000000.0

def rms_norm(values, gain):
    wide = values.astype(jnp.float32)
    square_mean = lax.optimization_barrier(jnp.mean(wide * wide, axis=-1, keepdims=True))
    return (wide * lax.rsqrt(square_mean + EPSILON) * gain.astype(jnp.float32)).astype(jnp.bfloat16)

def rope_angles(positions, head_dim):
    half_dim = head_dim // 2
    freqs = jnp.exp(jnp.arange(half_dim, dtype=jnp.float32) * (-2.0 * math.log(ROPE_BASE) / head_dim))
    return positions[:, None] * freqs[None, :]

def rotate(tensor, angles):
    half_dim = tensor.shape[-1] // 2
    first_half = tensor[..., :half_dim]
    second_half = tensor[..., half_dim:]
    cosine = jnp.cos(angles)
    sine = jnp.sin(angles)
    return jnp.concatenate([first_half * cosine - second_half * sine, second_half * cosine + first_half * sine], axis=-1)

def head_attend(operands):
    head_query_rows, head_key_rows, head_value_rows = operands
    length = head_key_rows.shape[1]
    score_matrix = jnp.einsum('ezjf,euf->ejzu', head_query_rows.astype(jnp.float32), head_key_rows.astype(jnp.float32)) * (1.0 / math.sqrt(HEAD_SIZE))
    causal = jnp.arange(length)[None, :] <= jnp.arange(length)[:, None]
    score_matrix = jnp.where(causal, score_matrix, -1e+30)
    peak = lax.optimization_barrier(jnp.max(score_matrix, axis=-1, keepdims=True))
    probs = jnp.where(causal, jnp.exp(score_matrix - peak), 0.0)
    totals = lax.optimization_barrier(jnp.sum(probs, axis=-1))
    rounded_result = lax.optimization_barrier(probs.astype(jnp.bfloat16)).astype(jnp.float32)
    summed_result = jnp.einsum('cszt,ctj->czsj', rounded_result, head_value_rows.astype(jnp.float32))
    return summed_result / jnp.transpose(totals, (0, 2, 1))[..., None]

def expert_apply(operands):
    rows_in, gate_up_e, down_e = operands
    mixed_proj = jnp.dot(rows_in, gate_up_e.reshape(D, 2 * FF_WIN), preferred_element_type=jnp.float32)
    mixed_proj = mixed_proj.reshape(-1, 2, FF_WIN)
    hidden = (jax.nn.silu(mixed_proj[:, 0]) * mixed_proj[:, 1]).astype(jnp.bfloat16)
    total = jnp.zeros((rows_in.shape[0], D), jnp.float32)
    for run in range(FF_WIN // FF_DEV):
        term = jnp.dot(hidden[:, run * FF_DEV:(run + 1) * FF_DEV], down_e[run * FF_DEV:(run + 1) * FF_DEV], preferred_element_type=jnp.float32)
        total = total + lax.optimization_barrier(term.astype(jnp.bfloat16)).astype(jnp.float32)
    return total.astype(jnp.bfloat16)

def reference(tokens, norm_in, w_qkv, w_out, norm_mid, w_router, w_gate_up, w_down, expert_ids, slot_index):
    batch = tokens.shape[0]
    length = tokens.shape[1]
    normed = rms_norm(tokens, norm_in)
    projected = jnp.dot(normed.reshape(batch * length, D), w_qkv.reshape(D, -1), preferred_element_type=jnp.float32)
    projected = projected.reshape(batch, length, KV_HEADS, GROUP + 2, HEAD_SIZE)
    angles = rope_angles(jnp.arange(length).astype(jnp.float32), HEAD_SIZE)
    queries = rotate(projected[:, :, :, :GROUP, :], angles[None, :, None, None, :]).astype(jnp.bfloat16)
    keys_rot = rotate(projected[:, :, :, GROUP, :], angles[None, :, None, :]).astype(jnp.bfloat16)
    values = projected[:, :, :, GROUP + 1, :].astype(jnp.bfloat16)
    attended = lax.map(head_attend, (jnp.moveaxis(queries, 2, 0), jnp.moveaxis(keys_rot, 2, 0), jnp.moveaxis(values, 2, 0)))
    attended = jnp.moveaxis(attended, 0, 2).astype(jnp.bfloat16)
    head_total = jnp.dot(attended.reshape(batch * length, HEADS * HEAD_SIZE), w_out.reshape(HEADS * HEAD_SIZE, D), preferred_element_type=jnp.float32)
    mixed = (tokens.reshape(batch * length, D).astype(jnp.float32) + head_total).astype(jnp.bfloat16)
    normed_mid = rms_norm(mixed, norm_mid)
    logits = jnp.dot(normed_mid, w_router, preferred_element_type=jnp.float32)
    flat_ids = expert_ids.reshape(batch * length, 2)
    chosen = jnp.take_along_axis(logits, flat_ids, axis=1)
    gate_first = 1.0 / (1.0 + jnp.exp(chosen[:, 1] - chosen[:, 0]))
    gate_second = 1.0 - gate_first
    block_count = batch * length // MOE_ROWS
    flat_index = (flat_ids * CAP + slot_index.reshape(batch * length, 2)).reshape(block_count, MOE_ROWS, 2)
    slot_cols = jnp.arange(EXPERTS * CAP).astype(jnp.int32)
    placer = jnp.logical_or(slot_cols[None, :, None] == flat_index[:, None, :, 0], slot_cols[None, :, None] == flat_index[:, None, :, 1]).astype(jnp.float32)
    block_rows = normed_mid.reshape(block_count, MOE_ROWS, D).astype(jnp.float32)
    buffers = jnp.einsum('bcr,brd->bcd', placer, block_rows, precision=lax.Precision.HIGHEST).astype(jnp.bfloat16)
    expert_rows = jnp.transpose(buffers.reshape(block_count, EXPERTS, CAP, D), (1, 0, 2, 3)).reshape(EXPERTS, block_count * CAP, D)
    expert_out = lax.map(expert_apply, (expert_rows, w_gate_up, w_down))
    expert_out = jnp.transpose(expert_out.reshape(EXPERTS, block_count, CAP, D), (1, 0, 2, 3)).reshape(block_count, EXPERTS * CAP, D)
    gate_first_b = gate_first.reshape(block_count, MOE_ROWS, 1)
    gate_second_b = gate_second.reshape(block_count, MOE_ROWS, 1)
    combiner = gate_first_b * (flat_index[:, :, 0:1] == slot_cols[None, None, :]).astype(jnp.float32) + gate_second_b * (flat_index[:, :, 1:2] == slot_cols[None, None, :]).astype(jnp.float32)
    moe_total = jnp.einsum('brc,bcd->brd', combiner, expert_out.astype(jnp.float32), precision=lax.Precision.HIGHEST)
    result = mixed.astype(jnp.float32) + moe_total.reshape(batch * length, D)
    return result.astype(jnp.bfloat16).reshape(batch, length, D)
```

```python
import math

import jax
import jax.numpy as jnp
from jax import lax
from jax.sharding import Mesh
from jax.sharding import PartitionSpec as P

EPSILON = 1e-05
ROPE_BASE = 1000000.0
F32 = jnp.float32
BF16 = jnp.bfloat16
SWAP = [(0, 1), (1, 0)]
CHIPS = ("yh", "x")


def rope_angles(positions, head_dim):
    half_dim = head_dim // 2
    freqs = jnp.exp(jnp.arange(half_dim, dtype=F32) * (-2.0 * math.log(ROPE_BASE) / head_dim))
    return positions[:, None] * freqs[None, :]


def rotate(tensor, angles):
    half_dim = tensor.shape[-1] // 2
    first_half = tensor[..., :half_dim]
    second_half = tensor[..., half_dim:]
    cosine = jnp.cos(angles)
    sine = jnp.sin(angles)
    return jnp.concatenate(
        [first_half * cosine - second_half * sine, second_half * cosine + first_half * sine],
        axis=-1,
    )


def swap_dp(array):
    return lax.ppermute(array, "dp", SWAP)


def swap_core(array):
    return lax.ppermute(array, "core", SWAP)


def forward_pairs(step_y, step_x):
    return [
        (y * 4 + x, (y ^ step_y) * 4 + (x + step_x) % 4) for y in range(2) for x in range(4)
    ]


def backward_pairs(step_y, step_x):
    return [(b, a) for a, b in forward_pairs(step_y, step_x)]


STEPS = [(0, 0), (1, 0), (0, 1), (0, 3), (1, 1), (1, 3), (0, 2), (1, 2)]


def halves(array, part):
    size = array.shape[-1] // 2
    own = lax.dynamic_slice_in_dim(array, part * size, size, array.ndim - 1)
    other = lax.dynamic_slice_in_dim(array, (1 - part) * size, size, array.ndim - 1)
    return own, other


def on_device(
    tokens, norm_in, w_qkv, w_out, norm_mid, w_router, w_gate_up, w_down, expert_ids, slot_index
):
    part = lax.axis_index("dp")
    core = lax.axis_index("core")
    chip = lax.axis_index("yh") * 4 + lax.axis_index("x")
    tok_rows = tokens.shape[1]
    width = tokens.shape[2]
    half = width // 2
    head_dim = w_qkv.shape[3]
    group_size = w_qkv.shape[2] - 2

    wide = tokens[0].astype(F32)
    scale_in = lax.rsqrt(jnp.mean(wide * wide, axis=-1, keepdims=True) + EPSILON)
    normed = (wide * scale_in * norm_in.astype(F32)).astype(BF16)
    normed_own, normed_other = halves(normed, part)
    normed_peer = swap_dp(normed_other)
    weights_in = w_qkv.reshape(half, -1)
    to_peer = jnp.dot(normed_peer, weights_in, preferred_element_type=F32).astype(BF16)
    from_peer = swap_dp(to_peer)
    projected = jnp.dot(normed_own, weights_in, preferred_element_type=F32) + from_peer.astype(F32)
    projected = projected.reshape(tok_rows, group_size + 2, head_dim)

    gate_up_own, down_own, _ = lax.optimization_barrier((w_gate_up[0], w_down[0], from_peer))
    gate_up_other = swap_dp(gate_up_own)
    down_other = swap_dp(down_own)

    query_idx = (chip * 2 + core) * tok_rows + jnp.arange(tok_rows, dtype=jnp.int32)
    angles = rope_angles(query_idx.astype(F32), head_dim)
    queries = rotate(projected[:, :group_size], angles[:, None, :]).astype(BF16)
    keys_rot = rotate(projected[:, group_size], angles).astype(BF16)
    values = projected[:, group_size + 1].astype(BF16)

    keys_values = jnp.concatenate([keys_rot, values], axis=-1)
    pieces = [keys_values] + [
        lax.ppermute(keys_values, CHIPS, [(i, i + step) for i in range(8 - step)])
        for step in range(1, 8)
    ]
    same_core = jnp.stack(pieces)
    all_pieces = jnp.stack([same_core, swap_core(same_core)])
    step_idx = jnp.arange(8, dtype=jnp.int32)[None, :, None]
    parity = jnp.stack([core, 1 - core])[:, None, None]
    key_idx = (
        ((chip - step_idx) * 2 + parity) * tok_rows
        + jnp.arange(tok_rows, dtype=jnp.int32)[None, None, :]
    ).reshape(-1)
    count = key_idx.shape[0]
    all_keys = all_pieces[..., :head_dim].reshape(count, head_dim)
    all_values = all_pieces[..., head_dim:].reshape(count, head_dim)
    scores = jnp.einsum("qgd,sd->gqs", queries, all_keys, preferred_element_type=F32) * (
        1.0 / math.sqrt(head_dim)
    )
    causal = jnp.logical_and(key_idx[None, :] <= query_idx[:, None], key_idx[None, :] >= 0)
    scores = jnp.where(causal, scores, -1e30)
    peak = jnp.max(scores, axis=-1, keepdims=True)
    probs = jnp.where(causal, jnp.exp(scores - peak), 0.0)
    totals = jnp.sum(probs, axis=-1)
    accum = jnp.einsum("gqs,sd->gqd", probs.astype(BF16), all_values, preferred_element_type=F32)
    attended = jnp.transpose(accum / totals[..., None], (1, 0, 2)).astype(BF16)
    attended = attended.reshape(tok_rows, group_size * head_dim)

    both = jnp.stack([attended, swap_dp(attended)])
    partial_sum = jnp.einsum(
        "bth,hd->btd", both, w_out.reshape(-1, half), preferred_element_type=F32
    ).astype(BF16)
    summed = lax.psum_scatter(partial_sum, "exp", scatter_dimension=1, tiled=True)
    rows = summed.shape[1]
    head_total = jnp.concatenate([summed[0], swap_dp(summed[1])], axis=-1).astype(F32)
    own_tokens = lax.dynamic_slice_in_dim(tokens[0], lax.axis_index("exp") * rows, rows, 0)
    own_tokens = jnp.concatenate(halves(own_tokens, part), axis=-1)
    mixed = (own_tokens.astype(F32) + head_total).astype(BF16)

    wide_mid = mixed.astype(F32)
    scale_mid = lax.rsqrt(jnp.mean(wide_mid * wide_mid, axis=-1, keepdims=True) + EPSILON)
    gain_mid = jnp.concatenate(halves(norm_mid, part), axis=-1).astype(F32)
    normed_mid = (wide_mid * scale_mid * gain_mid).astype(BF16)
    router = jnp.concatenate(
        [
            lax.dynamic_slice_in_dim(w_router, part * half, half, 0),
            lax.dynamic_slice_in_dim(w_router, (1 - part) * half, half, 0),
        ],
        axis=0,
    )
    logits = jnp.dot(normed_mid, router, preferred_element_type=F32)
    expert_count = w_router.shape[1]
    choice_ids = expert_ids[0]
    picks = choice_ids[:, :, None] == jnp.arange(expert_count, dtype=jnp.int32)[None, None, :]
    chosen = jnp.sum(jnp.where(picks, logits[:, None, :], 0.0), axis=-1)
    gate_first = 1.0 / (1.0 + jnp.exp(chosen[:, 1] - chosen[:, 0]))
    gate_second = 1.0 - gate_first
    capacity = 6
    flat_index = choice_ids * capacity + slot_index[0]
    slot_cols = jnp.arange(expert_count * capacity, dtype=jnp.int32)
    placer = jnp.logical_or(
        slot_cols[:, None] == flat_index[None, :, 0], slot_cols[:, None] == flat_index[None, :, 1]
    ).astype(BF16)
    buffer_rows = jnp.dot(placer, normed_mid, preferred_element_type=F32).astype(BF16)
    buffer_rows = buffer_rows.reshape(expert_count, capacity, width)
    received = lax.all_to_all(buffer_rows, "exp", split_axis=0, concat_axis=0, tiled=True)
    received = received.reshape(expert_count * capacity, width)

    same_core_rows = jnp.stack(
        [received] + [lax.ppermute(received, CHIPS, forward_pairs(*s)) for s in STEPS[1:]]
    )
    expert_rows = jnp.stack([same_core_rows, swap_core(same_core_rows)]).reshape(-1, width)
    gate_up = jnp.einsum(
        "rd,djf->rjf", expert_rows[:, :half], gate_up_own, preferred_element_type=F32
    ) + jnp.einsum("rd,djf->rjf", expert_rows[:, half:], gate_up_other, preferred_element_type=F32)
    hidden = (jax.nn.silu(gate_up[:, 0]) * gate_up[:, 1]).astype(BF16)
    down = jnp.concatenate(
        [
            jnp.dot(hidden, down_own, preferred_element_type=F32).astype(BF16),
            jnp.dot(hidden, down_other, preferred_element_type=F32).astype(BF16),
        ],
        axis=-1,
    ).reshape(2, 8, expert_count * capacity, width)

    pair_sum = (down[0].astype(F32) + swap_core(down[1]).astype(F32)).astype(BF16)
    total = pair_sum[0].astype(F32)
    for index, step in enumerate(STEPS[1:]):
        total = total + lax.ppermute(pair_sum[index + 1], CHIPS, backward_pairs(*step)).astype(F32)
    expert_out = total.astype(BF16).reshape(expert_count, capacity, width)
    returned = lax.all_to_all(expert_out, "exp", split_axis=0, concat_axis=0, tiled=True)
    returned = returned.reshape(expert_count * capacity, width)
    combiner = gate_first[:, None] * (flat_index[:, 0:1] == slot_cols[None, :]).astype(
        F32
    ) + gate_second[:, None] * (flat_index[:, 1:2] == slot_cols[None, :]).astype(F32)
    moe_total = jnp.dot(combiner, returned.astype(F32), precision=lax.Precision.HIGHEST)
    layer_out = (mixed.astype(F32) + moe_total).astype(BF16)
    return jnp.concatenate(halves(layer_out, part), axis=-1)[None]


def solution(mesh):
    fine = Mesh(mesh.devices.reshape(2, 4, 2, 8, 2), ("yh", "x", "core", "exp", "dp"))
    ctx = ("yh", "x", "core")
    rows = ctx + ("exp",)
    placed = (
        P("dp", ctx, None),
        P(),
        P("dp", "exp", None, None),
        P("exp", None, None, "dp"),
        P(),
        P(),
        P("exp", "dp", None, ctx),
        P("exp", ctx, "dp"),
        P("dp", rows, None),
        P("dp", rows, None),
    )
    return jax.shard_map(
        on_device,
        mesh=fine,
        in_specs=placed,
        out_specs=P("dp", rows, None),
        check_vma=False,
    )
```

```python
import math

import jax
import jax.numpy as jnp
from jax import lax
from jax.sharding import Mesh
from jax.sharding import PartitionSpec as P

EPSILON = 1e-05
ROPE_BASE = 1000000.0
F32 = jnp.float32
BF16 = jnp.bfloat16
SWAP = [(0, 1), (1, 0)]
CHIPS = ("yh", "x")


def rope_angles(positions, head_dim):
    half_dim = head_dim // 2
    freqs = jnp.exp(jnp.arange(half_dim, dtype=F32) * (-2.0 * math.log(ROPE_BASE) / head_dim))
    return positions[:, None] * freqs[None, :]


def rotate(tensor, angles):
    half_dim = tensor.shape[-1] // 2
    first_half = tensor[..., :half_dim]
    second_half = tensor[..., half_dim:]
    cosine = jnp.cos(angles)
    sine = jnp.sin(angles)
    return jnp.concatenate(
        [first_half * cosine - second_half * sine, second_half * cosine + first_half * sine],
        axis=-1,
    )


def swap_dp(array):
    return lax.ppermute(array, "dp", SWAP)


def swap_core(array):
    return lax.ppermute(array, "core", SWAP)


def forward_pairs(step_y, step_x):
    return [
        (y * 4 + x, (y ^ step_y) * 4 + (x + step_x) % 4) for y in range(2) for x in range(4)
    ]


def backward_pairs(step_y, step_x):
    return [(b, a) for a, b in forward_pairs(step_y, step_x)]


GROUPS = [[(0, 0), (1, 0), (0, 1), (0, 3)], [(1, 1), (1, 3), (0, 2), (1, 2)]]


def halves(array, part):
    size = array.shape[-1] // 2
    own = lax.dynamic_slice_in_dim(array, part * size, size, array.ndim - 1)
    other = lax.dynamic_slice_in_dim(array, (1 - part) * size, size, array.ndim - 1)
    return own, other


def ring_sum_exp(terms):
    count = 8
    place = lax.axis_index("exp")
    terms = terms.reshape(terms.shape[0], count, -1, terms.shape[-1])

    def own(offset):
        index = lax.rem(place + offset + count, count)
        return lax.dynamic_index_in_dim(terms, index, 1, keepdims=False)

    up_pairs = [(i, (i + 1) % count) for i in range(count)]
    down_pairs = [(i, (i + count - 1) % count) for i in range(count)]
    up, down = own(4), own(-3)
    for step in range(4):
        up = lax.ppermute(up, "exp", up_pairs)
        if step < 3:
            up = (up.astype(F32) + own(3 - step).astype(F32)).astype(BF16)
            down = lax.ppermute(down, "exp", down_pairs)
            if step < 2:
                down = (down.astype(F32) + own(step - 2).astype(F32)).astype(BF16)
    return (up.astype(F32) + down.astype(F32) + own(0).astype(F32)).astype(BF16)


def on_device(
    tokens, norm_in, w_qkv, w_out, norm_mid, w_router, w_gate_up, w_down, expert_ids, slot_index
):
    part = lax.axis_index("dp")
    core = lax.axis_index("core")
    chip = lax.axis_index("yh") * 4 + lax.axis_index("x")
    tok_rows = tokens.shape[1]
    width = tokens.shape[2]
    half = width // 2
    head_dim = w_qkv.shape[3]
    group_size = w_qkv.shape[2] - 2

    wide = tokens[0].astype(F32)
    scale_in = lax.rsqrt(jnp.mean(wide * wide, axis=-1, keepdims=True) + EPSILON)
    normed = (wide * scale_in * norm_in.astype(F32)).astype(BF16)
    normed_own, normed_other = halves(normed, part)
    normed_peer = swap_dp(normed_other)
    weights_in = w_qkv.reshape(half, -1)
    to_peer = jnp.dot(normed_peer, weights_in, preferred_element_type=F32).astype(BF16)
    from_peer = swap_dp(to_peer)
    projected = jnp.dot(normed_own, weights_in, preferred_element_type=F32) + from_peer.astype(F32)
    projected = projected.reshape(tok_rows, group_size + 2, head_dim)

    gate_up_full = lax.all_gather(w_gate_up[0], "dp", axis=0, tiled=True)
    down_mate = swap_core(w_down[0])

    query_idx = (chip * 2 + core) * tok_rows + jnp.arange(tok_rows, dtype=jnp.int32)
    angles = rope_angles(query_idx.astype(F32), head_dim)
    queries = rotate(projected[:, :group_size], angles[:, None, :]).astype(BF16)
    keys_rot = rotate(projected[:, group_size], angles).astype(BF16)
    values = projected[:, group_size + 1].astype(BF16)

    keys_values = jnp.concatenate([keys_rot, values], axis=-1)
    pieces = [keys_values] + [
        lax.ppermute(keys_values, CHIPS, [(i, i + step) for i in range(8 - step)])
        for step in range(1, 8)
    ]
    same_core = jnp.stack(pieces)
    all_pieces = jnp.stack([same_core, swap_core(same_core)])
    step_idx = jnp.arange(8, dtype=jnp.int32)[None, :, None]
    parity = jnp.stack([core, 1 - core])[:, None, None]
    key_idx = (
        ((chip - step_idx) * 2 + parity) * tok_rows
        + jnp.arange(tok_rows, dtype=jnp.int32)[None, None, :]
    ).reshape(-1)
    count = key_idx.shape[0]
    all_keys = all_pieces[..., :head_dim].reshape(count, head_dim)
    all_values = all_pieces[..., head_dim:].reshape(count, head_dim)
    scores = jnp.einsum("qgd,sd->gqs", queries, all_keys, preferred_element_type=F32) * (
        1.0 / math.sqrt(head_dim)
    )
    causal = jnp.logical_and(key_idx[None, :] <= query_idx[:, None], key_idx[None, :] >= 0)
    scores = jnp.where(causal, scores, -1e30)
    peak = jnp.max(scores, axis=-1, keepdims=True)
    probs = jnp.where(causal, jnp.exp(scores - peak), 0.0)
    totals = jnp.sum(probs, axis=-1)
    accum = jnp.einsum("gqs,sd->gqd", probs.astype(BF16), all_values, preferred_element_type=F32)
    attended = jnp.transpose(accum / totals[..., None], (1, 0, 2)).astype(BF16)
    attended = attended.reshape(tok_rows, group_size * head_dim)

    both = jnp.stack([attended, swap_dp(attended)])
    partial_sum = jnp.einsum(
        "bth,hd->btd", both, w_out.reshape(-1, half), preferred_element_type=F32
    ).astype(BF16)
    summed = ring_sum_exp(partial_sum)
    rows = summed.shape[1]
    head_total = jnp.concatenate([summed[0], swap_dp(summed[1])], axis=-1)
    head_total = jnp.concatenate(halves(head_total, part), axis=-1).astype(F32)
    own_tokens = lax.dynamic_slice_in_dim(tokens[0], lax.axis_index("exp") * rows, rows, 0)
    mixed = (own_tokens.astype(F32) + head_total).astype(BF16)

    wide_mid = mixed.astype(F32)
    scale_mid = lax.rsqrt(jnp.mean(wide_mid * wide_mid, axis=-1, keepdims=True) + EPSILON)
    normed_mid = (wide_mid * scale_mid * norm_mid.astype(F32)).astype(BF16)
    logits = jnp.dot(normed_mid, w_router, preferred_element_type=F32)
    expert_count = w_router.shape[1]
    choice_ids = expert_ids[0]
    picks = choice_ids[:, :, None] == jnp.arange(expert_count, dtype=jnp.int32)[None, None, :]
    chosen = jnp.sum(jnp.where(picks, logits[:, None, :], 0.0), axis=-1)
    gate_first = 1.0 / (1.0 + jnp.exp(chosen[:, 1] - chosen[:, 0]))
    gate_second = 1.0 - gate_first
    capacity = 6
    flat_index = choice_ids * capacity + slot_index[0]
    slot_cols = jnp.arange(expert_count * capacity, dtype=jnp.int32)
    combiner = gate_first[:, None] * (flat_index[:, 0:1] == slot_cols[None, :]).astype(
        F32
    ) + gate_second[:, None] * (flat_index[:, 1:2] == slot_cols[None, :]).astype(F32)
    combiners = jnp.stack([combiner, swap_dp(combiner)])
    placer = jnp.logical_or(
        slot_cols[:, None] == flat_index[None, :, 0], slot_cols[:, None] == flat_index[None, :, 1]
    ).astype(BF16)
    buffer_rows = jnp.dot(placer, normed_mid, preferred_element_type=F32).astype(BF16)
    buffer_rows = buffer_rows.reshape(expert_count, capacity, width)
    received = lax.all_to_all(buffer_rows, "exp", split_axis=0, concat_axis=0, tiled=True)
    received = received.reshape(expert_count * capacity, width)
    received, gate_up_full = lax.optimization_barrier((received, gate_up_full))
    gate_up_mate = swap_core(gate_up_full)

    hidden_groups = []
    for group in GROUPS:
        pieces = [
            lax.ppermute(received, CHIPS, forward_pairs(*step)) if step != (0, 0) else received
            for step in group
        ]
        group_rows = jnp.concatenate(pieces)
        parts = []
        for weights in (gate_up_full, gate_up_mate):
            gate_up = jnp.einsum("rd,djf->rjf", group_rows, weights, preferred_element_type=F32)
            parts.append((jax.nn.silu(gate_up[:, 0]) * gate_up[:, 1]).astype(BF16))
        hidden_groups.append(jnp.concatenate(parts, axis=-1))

    down_both = jnp.concatenate([w_down[0], down_mate])
    total = 0.0
    for group, hidden in zip(GROUPS, hidden_groups):
        hidden = jnp.stack([hidden, swap_dp(hidden)])
        down = jnp.einsum(
            "prf,fd->prd", hidden, down_both, preferred_element_type=F32
        ).astype(BF16)
        for index, step in enumerate(group):
            piece = down[:, index * 48 : (index + 1) * 48]
            if step != (0, 0):
                piece = lax.ppermute(piece, CHIPS, backward_pairs(*step))
            total = total + piece.astype(F32)
    expert_out = total.astype(BF16).reshape(2, expert_count, capacity, half)
    returned = lax.all_to_all(expert_out, "exp", split_axis=1, concat_axis=1, tiled=True)
    returned = returned.reshape(2, expert_count * capacity, half)
    moe_both = jnp.einsum(
        "prc,pcd->prd", combiners, returned.astype(F32), precision=lax.Precision.HIGHEST
    )
    moe_total = jnp.concatenate(
        [moe_both[0], swap_dp(moe_both[1].astype(BF16)).astype(F32)], axis=-1
    )
    moe_total = jnp.concatenate(halves(moe_total, part), axis=-1)
    return (mixed.astype(F32) + moe_total).astype(BF16)[None]


def solution(mesh):
    fine = Mesh(mesh.devices.reshape(2, 4, 2, 8, 2), ("yh", "x", "core", "exp", "dp"))
    ctx = ("yh", "x", "core")
    rows = ctx + ("exp",)
    placed = (
        P("dp", ctx, None),
        P(),
        P("dp", "exp", None, None),
        P("exp", None, None, "dp"),
        P(),
        P(),
        P("exp", "dp", None, ctx),
        P("exp", ctx, "dp"),
        P("dp", rows, None),
        P("dp", rows, None),
    )
    return jax.shard_map(
        on_device,
        mesh=fine,
        in_specs=placed,
        out_specs=P("dp", rows, None),
        check_vma=False,
    )
```

```python
import math

import jax
import jax.numpy as jnp
from jax import lax
from jax.experimental import pallas as pl
from jax.experimental.pallas import tpu as pltpu
from jax.sharding import Mesh
from jax.sharding import PartitionSpec as P

EPSILON = 1e-05
ROPE_BASE = 1000000.0
F32 = jnp.float32
BF16 = jnp.bfloat16
SWAP = [(0, 1), (1, 0)]
CHIPS = ("yh", "x")


def rope_angles(positions, head_dim):
    half_dim = head_dim // 2
    freqs = jnp.exp(jnp.arange(half_dim, dtype=F32) * (-2.0 * math.log(ROPE_BASE) / head_dim))
    return positions[:, None] * freqs[None, :]


def rotary_kernel(own_ref, peer_ref, cosine_ref, sine_ref, queries_ref, keys_values_ref):
    size = cosine_ref.shape[1]
    group = queries_ref.shape[1] // size
    cosine, sine = cosine_ref[...], sine_ref[...]

    def projected(index):
        columns = slice(index * size, (index + 1) * size)
        return own_ref[:, columns] + peer_ref[:, columns].astype(F32)

    def rotated(index):
        value = projected(index)
        turned = jnp.concatenate([value[:, size // 2 :], value[:, : size // 2]], axis=1)
        return (value * cosine + turned * sine).astype(BF16)

    for index in range(group):
        queries_ref[:, index * size : (index + 1) * size] = rotated(index)
    keys_values_ref[:, :size] = rotated(group)
    keys_values_ref[:, size:] = projected(group + 1).astype(BF16)


def rotary(own, peer, cosine, sine):
    rows, size = cosine.shape
    group = own.shape[1] // size - 2
    return pl.pallas_call(
        rotary_kernel,
        out_shape=(
            jax.ShapeDtypeStruct((rows, group * size), BF16),
            jax.ShapeDtypeStruct((rows, 2 * size), BF16),
        ),
        in_specs=[pl.BlockSpec(memory_space=pltpu.VMEM)] * 4,
        out_specs=[pl.BlockSpec(memory_space=pltpu.VMEM)] * 2,
        cost_estimate=pl.CostEstimate(
            flops=own.size * 4, bytes_accessed=own.size * 8, transcendentals=0
        ),
        name="rotary",
    )(own, peer, cosine, sine)


def attention_kernel(place_ref, queries_ref, mine_ref, mates_ref, out_ref):
    chip, core = place_ref[0], place_ref[1]
    rows = queries_ref.shape[0]
    size = mine_ref.shape[1] // 2
    query_pos = (chip * 2 + core) * rows + lax.broadcasted_iota(jnp.int32, (rows, 1), 0)

    def valid_keys(count, lead, parity, first_piece):
        column = lax.broadcasted_iota(jnp.int32, (1, count), 1)
        piece = column // (2 * rows)
        half_of = (column // rows) % 2
        back = jnp.where(piece < lead, 0, piece + (first_piece - lead))
        side = jnp.where(half_of == 0, parity, 1 - parity)
        key_pos = ((chip - back) * 2 + side) * rows + column % rows
        return jnp.logical_and(key_pos >= 0, key_pos <= query_pos)

    sides = (
        (mine_ref, valid_keys(mine_ref.shape[0], 1, core, 1 + 4 * core)),
        (mates_ref, valid_keys(mates_ref.shape[0], 0, 1 - core, 5 - 4 * core)),
    )
    scale = 1.0 / math.sqrt(size)
    contract_last = (((1,), (1,)), ((), ()))
    for head in range(queries_ref.shape[1] // size):
        query = queries_ref[:, head * size : (head + 1) * size]
        scores = [
            jnp.where(
                valid,
                scale
                * lax.dot_general(
                    query, ref[:, :size], contract_last, preferred_element_type=F32
                ),
                -1e30,
            )
            for ref, valid in sides
        ]
        peak = jnp.maximum(
            jnp.max(scores[0], axis=1, keepdims=True), jnp.max(scores[1], axis=1, keepdims=True)
        )
        total, accum = 0.0, 0.0
        for (ref, valid), score in zip(sides, scores):
            probs = jnp.where(valid, jnp.exp(score - peak), 0.0)
            total = total + jnp.sum(probs, axis=1, keepdims=True)
            accum = accum + jnp.dot(
                probs.astype(BF16), ref[:, size:], preferred_element_type=F32
            )
        out_ref[:, head * size : (head + 1) * size] = (accum / total).astype(BF16)


def attention(place, queries, mine, mates):
    vmem = pl.BlockSpec(memory_space=pltpu.VMEM)
    return pl.pallas_call(
        attention_kernel,
        out_shape=jax.ShapeDtypeStruct(queries.shape, BF16),
        in_specs=[pl.BlockSpec(memory_space=pltpu.SMEM), vmem, vmem, vmem],
        out_specs=vmem,
        cost_estimate=pl.CostEstimate(
            flops=queries.size * 4 * (mine.shape[0] + mates.shape[0]),
            bytes_accessed=2 * (2 * queries.size + mine.size + mates.size),
            transcendentals=queries.size // (mine.shape[1] // 2) * (mine.shape[0] + mates.shape[0]),
        ),
        compiler_params=pltpu.CompilerParams(vmem_limit_bytes=24 * 2**20),
        name="attention",
    )(place, queries, mine, mates)


def swap_dp(array):
    return lax.ppermute(array, "dp", SWAP)


def swap_core(array):
    return lax.ppermute(array, "core", SWAP)


FLIP_Y, RIGHT, LEFT, ACROSS = (1, 0), (0, 1), (0, 3), (0, 2)


def hop(array, even=None, odd=None):
    pairs = []
    for core, step in enumerate((even, odd)):
        if step is not None:
            for y in range(2):
                for x in range(4):
                    target = (y ^ step[0]) * 4 + (x + step[1]) % 4
                    pairs.append(((y * 4 + x) * 2 + core, target * 2 + core))
    return lax.ppermute(array, ("yh", "x", "core"), pairs)


def halves(array, part):
    size = array.shape[-1] // 2
    own = lax.dynamic_slice_in_dim(array, part * size, size, array.ndim - 1)
    other = lax.dynamic_slice_in_dim(array, (1 - part) * size, size, array.ndim - 1)
    return own, other


def ring_sum_exp(terms):
    count = 8
    terms = terms.reshape(terms.shape[0], count, -1, terms.shape[-1])

    def own(offset):
        return terms[:, offset % count]

    up_pairs = [(i, (i + 1) % count) for i in range(count)]
    down_pairs = [(i, (i + count - 1) % count) for i in range(count)]
    up, down = own(4), own(-3)
    for step in range(4):
        up = lax.ppermute(up, "exp", up_pairs)
        if step < 3:
            up = (up.astype(F32) + own(3 - step).astype(F32)).astype(BF16)
            down = lax.ppermute(down, "exp", down_pairs)
            if step < 2:
                down = (down.astype(F32) + own(step - 2).astype(F32)).astype(BF16)
    return (up.astype(F32) + down.astype(F32) + own(0).astype(F32)).astype(BF16)


def on_device(
    tokens, norm_in, w_qkv, w_out, norm_mid, w_router, w_gate_up, w_down, expert_ids, slot_index
):
    part = lax.axis_index("dp")
    core = lax.axis_index("core")
    chip = lax.axis_index("yh") * 4 + lax.axis_index("x")
    tok_rows = tokens.shape[1]
    width = tokens.shape[2]
    half = width // 2
    head_dim = w_qkv.shape[3]

    tokens_own, tokens_other = halves(tokens[0], part)
    tokens_peer = swap_dp(tokens_other)
    wide = tokens[0].astype(F32)
    scale_in = lax.rsqrt(jnp.mean(wide * wide, axis=-1) + EPSILON)
    scale_peer = swap_dp(scale_in[None])[0]
    gain_own = halves(norm_in, part)[0].astype(F32)
    normed_own = (tokens_own.astype(F32) * scale_in[:, None] * gain_own).astype(BF16)
    normed_peer = (tokens_peer.astype(F32) * scale_peer[:, None] * gain_own).astype(BF16)
    weights_in = w_qkv.reshape(half, -1)
    to_peer = jnp.dot(normed_peer, weights_in, preferred_element_type=F32).astype(BF16)
    from_peer = swap_dp(to_peer)
    projected_own = jnp.dot(normed_own, weights_in, preferred_element_type=F32)

    gate_up_part, _ = lax.optimization_barrier((w_gate_up[0], (tokens_other, scale_in)))
    gate_up_full = lax.all_gather(gate_up_part, "dp", axis=0, tiled=True)

    query_idx = (chip * 2 + core) * tok_rows + jnp.arange(tok_rows, dtype=jnp.int32)
    angles = rope_angles(query_idx.astype(F32), head_dim)
    cosine, sine = jnp.cos(angles), jnp.sin(angles)
    queries, keys_values = rotary(
        projected_own,
        from_peer,
        jnp.concatenate([cosine, cosine], axis=1),
        jnp.concatenate([-sine, sine], axis=1),
    )

    pair = jnp.concatenate([keys_values, swap_core(keys_values)])
    pieces = []
    for step in range(1, 5):
        pairs = [(i * 2, (i + step) * 2) for i in range(8 - step)]
        pairs += [(i * 2 + 1, (i + step + 4) * 2 + 1) for i in range(4 - step)]
        pieces.append(lax.ppermute(pair, CHIPS + ("core",), pairs))
    earlier = jnp.concatenate(pieces)
    mates = swap_core(earlier)
    attended = attention(
        jnp.stack([chip, core]), queries, jnp.concatenate([pair, earlier]), mates
    )

    rows = tok_rows // 8
    attended = lax.dynamic_slice_in_dim(
        jnp.concatenate([attended, attended]), lax.axis_index("exp") * rows, tok_rows, 0
    )

    both = jnp.stack([attended, swap_dp(attended)])
    partial_sum = jnp.einsum(
        "bth,hd->btd", both, w_out.reshape(-1, half), preferred_element_type=F32
    ).astype(BF16)
    summed = ring_sum_exp(partial_sum)
    summed, down_mate = lax.optimization_barrier((summed, swap_core(w_down[0])))
    head_total = jnp.concatenate([summed[0], swap_dp(summed[1])], axis=-1)
    head_total = jnp.concatenate(halves(head_total, part), axis=-1).astype(F32)
    own_tokens = lax.dynamic_slice_in_dim(tokens[0], lax.axis_index("exp") * rows, rows, 0)
    mixed = (own_tokens.astype(F32) + head_total).astype(BF16)

    wide_mid = mixed.astype(F32)
    scale_mid = lax.rsqrt(jnp.mean(wide_mid * wide_mid, axis=-1, keepdims=True) + EPSILON)
    normed_mid = (wide_mid * scale_mid * norm_mid.astype(F32)).astype(BF16)
    logits = jnp.dot(normed_mid, w_router, preferred_element_type=F32)
    expert_count = w_router.shape[1]
    choice_ids = expert_ids[0]
    picks = choice_ids[:, :, None] == jnp.arange(expert_count, dtype=jnp.int32)[None, None, :]
    chosen = jnp.sum(jnp.where(picks, logits[:, None, :], 0.0), axis=-1)
    gate_first = 1.0 / (1.0 + jnp.exp(chosen[:, 1] - chosen[:, 0]))
    gate_second = 1.0 - gate_first
    capacity = 6
    flat_index = choice_ids * capacity + slot_index[0]
    slot_cols = jnp.arange(expert_count * capacity, dtype=jnp.int32)
    combiner = gate_first[:, None] * (flat_index[:, 0:1] == slot_cols[None, :]).astype(
        F32
    ) + gate_second[:, None] * (flat_index[:, 1:2] == slot_cols[None, :]).astype(F32)
    combiners = jnp.stack([combiner, swap_dp(combiner)])
    placer = jnp.logical_or(
        slot_cols[:, None] == flat_index[None, :, 0], slot_cols[:, None] == flat_index[None, :, 1]
    ).astype(BF16)
    buffer_rows = jnp.dot(placer, normed_mid, preferred_element_type=F32).astype(BF16)
    buffer_rows = buffer_rows.reshape(expert_count, capacity, width)
    received = lax.all_to_all(buffer_rows, "exp", split_axis=0, concat_axis=0, tiled=True)
    received = received.reshape(expert_count * capacity, width)

    first = core == 0
    from_1 = hop(received, even=FLIP_Y, odd=RIGHT)
    from_2 = hop(received, odd=LEFT)
    from_3 = hop(received, odd=ACROSS)
    near = jnp.concatenate([received, from_1])
    side = jnp.concatenate([from_2, from_3])
    near, side, gate_up_full = lax.optimization_barrier((near, side, gate_up_full))
    gate_up_mate = swap_core(gate_up_full)
    far_1 = hop(near, even=RIGHT, odd=FLIP_Y)
    far_2 = hop(jnp.where(first, near, side), even=LEFT, odd=FLIP_Y)
    far_3 = hop(near, even=ACROSS)
    expert_rows = jnp.concatenate([near, far_1, far_2, jnp.where(first, far_3, side)])
    down = 0.0
    for weights, down_part in ((gate_up_full, w_down[0]), (gate_up_mate, down_mate)):
        gate_up = jnp.einsum("rd,djf->rjf", expert_rows, weights, preferred_element_type=F32)
        hidden = (jax.nn.silu(gate_up[:, 0]) * gate_up[:, 1]).astype(BF16)
        hidden = jnp.stack([hidden, swap_dp(hidden)])
        down = down + jnp.einsum("prf,fd->prd", hidden, down_part, preferred_element_type=F32)
    down = down.astype(BF16)

    slots = expert_count * capacity
    res_near, res_1, res_2, res_3 = (
        down[:, i * 2 * slots : (i + 1) * 2 * slots] for i in range(4)
    )
    back_1 = hop(res_1, even=LEFT, odd=FLIP_Y).astype(F32)
    back_2 = hop(res_2, even=RIGHT, odd=FLIP_Y).astype(F32)
    back_3 = hop(res_3, even=ACROSS).astype(F32)
    sum_near = res_near.astype(F32) + back_1 + jnp.where(first, back_2, 0.0) + back_3
    sum_side = (res_3.astype(F32) + back_2).astype(BF16)
    total = (
        sum_near[:, :slots]
        + hop(sum_near[:, slots:].astype(BF16), even=FLIP_Y, odd=LEFT).astype(F32)
        + hop(sum_side[:, :slots], odd=RIGHT).astype(F32)
        + hop(sum_side[:, slots:], odd=ACROSS).astype(F32)
    )
    expert_out = total.astype(BF16).reshape(2, expert_count, capacity, half)
    returned = lax.all_to_all(expert_out, "exp", split_axis=1, concat_axis=1, tiled=True)
    returned = returned.reshape(2, expert_count * capacity, half)
    moe_both = jnp.einsum(
        "prc,pcd->prd", combiners, returned.astype(F32), precision=lax.Precision.HIGHEST
    )
    moe_total = jnp.concatenate(
        [moe_both[0], swap_dp(moe_both[1].astype(BF16)).astype(F32)], axis=-1
    )
    moe_total = jnp.concatenate(halves(moe_total, part), axis=-1)
    return (mixed.astype(F32) + moe_total).astype(BF16)[None]


def solution(mesh):
    fine = Mesh(mesh.devices.reshape(2, 4, 2, 8, 2), ("yh", "x", "core", "exp", "dp"))
    ctx = ("yh", "x", "core")
    rows = ctx + ("exp",)
    placed = (
        P("dp", ctx, None),
        P(),
        P("dp", "exp", None, None),
        P("exp", None, None, "dp"),
        P(),
        P(),
        P("exp", "dp", None, ctx),
        P("exp", ctx, "dp"),
        P("dp", rows, None),
        P("dp", rows, None),
    )
    return jax.shard_map(
        on_device,
        mesh=fine,
        in_specs=placed,
        out_specs=P("dp", rows, None),
        check_vma=False,
    )
```

```python
import math

import jax
import jax.numpy as jnp
from jax import lax
from jax.experimental import pallas as pl
from jax.experimental.pallas import tpu as pltpu
from jax.sharding import Mesh
from jax.sharding import PartitionSpec as P

EPSILON = 1e-05
ROPE_BASE = 1000000.0
F32 = jnp.float32
BF16 = jnp.bfloat16
SWAP = [(0, 1), (1, 0)]
CHIPS = ("yh", "x")


def rope_angles(positions, head_dim):
    half_dim = head_dim // 2
    freqs = jnp.exp(jnp.arange(half_dim, dtype=F32) * (-2.0 * math.log(ROPE_BASE) / head_dim))
    return positions[:, None] * freqs[None, :]


def rotary_kernel(own_ref, peer_ref, cosine_ref, sine_ref, queries_ref, keys_values_ref):
    size = cosine_ref.shape[1]
    group = queries_ref.shape[1] // size
    cosine, sine = cosine_ref[...], sine_ref[...]

    def projected(index):
        columns = slice(index * size, (index + 1) * size)
        return own_ref[:, columns] + peer_ref[:, columns].astype(F32)

    def rotated(index):
        value = projected(index)
        turned = jnp.concatenate([value[:, size // 2 :], value[:, : size // 2]], axis=1)
        return (value * cosine + turned * sine).astype(BF16)

    for index in range(group):
        queries_ref[:, index * size : (index + 1) * size] = rotated(index)
    keys_values_ref[:, :size] = rotated(group)
    keys_values_ref[:, size:] = projected(group + 1).astype(BF16)


def rotary(own, peer, cosine, sine):
    rows, size = cosine.shape
    group = own.shape[1] // size - 2
    return pl.pallas_call(
        rotary_kernel,
        out_shape=(
            jax.ShapeDtypeStruct((rows, group * size), BF16),
            jax.ShapeDtypeStruct((rows, 2 * size), BF16),
        ),
        in_specs=[pl.BlockSpec(memory_space=pltpu.VMEM)] * 4,
        out_specs=[pl.BlockSpec(memory_space=pltpu.VMEM)] * 2,
        cost_estimate=pl.CostEstimate(
            flops=own.size * 4, bytes_accessed=own.size * 8, transcendentals=0
        ),
        name="rotary",
    )(own, peer, cosine, sine)


def attention_kernel(place_ref, queries_ref, mine_ref, mates_ref, out_ref):
    chip, core = place_ref[0], place_ref[1]
    rows = queries_ref.shape[0]
    size = mine_ref.shape[1] // 2
    query_pos = (chip * 2 + core) * rows + lax.broadcasted_iota(jnp.int32, (rows, 1), 0)

    def valid_keys(count, lead, parity, first_piece):
        column = lax.broadcasted_iota(jnp.int32, (1, count), 1)
        piece = column // (2 * rows)
        half_of = (column // rows) % 2
        back = jnp.where(piece < lead, 0, piece + (first_piece - lead))
        side = jnp.where(half_of == 0, parity, 1 - parity)
        key_pos = ((chip - back) * 2 + side) * rows + column % rows
        return jnp.logical_and(key_pos >= 0, key_pos <= query_pos)

    sides = (
        (mine_ref, valid_keys(mine_ref.shape[0], 1, core, 1 + 4 * core)),
        (mates_ref, valid_keys(mates_ref.shape[0], 0, 1 - core, 5 - 4 * core)),
    )
    scale = 1.0 / math.sqrt(size)
    contract_last = (((1,), (1,)), ((), ()))
    for head in range(queries_ref.shape[1] // size):
        query = queries_ref[:, head * size : (head + 1) * size]
        scores = [
            jnp.where(
                valid,
                scale
                * lax.dot_general(
                    query, ref[:, :size], contract_last, preferred_element_type=F32
                ),
                -1e30,
            )
            for ref, valid in sides
        ]
        peak = jnp.maximum(
            jnp.max(scores[0], axis=1, keepdims=True), jnp.max(scores[1], axis=1, keepdims=True)
        )
        total, accum = 0.0, 0.0
        for (ref, valid), score in zip(sides, scores):
            probs = jnp.where(valid, jnp.exp(score - peak), 0.0)
            total = total + jnp.sum(probs, axis=1, keepdims=True)
            accum = accum + jnp.dot(
                probs.astype(BF16), ref[:, size:], preferred_element_type=F32
            )
        out_ref[:, head * size : (head + 1) * size] = (accum / total).astype(BF16)


def attention(place, queries, mine, mates):
    vmem = pl.BlockSpec(memory_space=pltpu.VMEM)
    return pl.pallas_call(
        attention_kernel,
        out_shape=jax.ShapeDtypeStruct(queries.shape, BF16),
        in_specs=[pl.BlockSpec(memory_space=pltpu.SMEM), vmem, vmem, vmem],
        out_specs=vmem,
        cost_estimate=pl.CostEstimate(
            flops=queries.size * 4 * (mine.shape[0] + mates.shape[0]),
            bytes_accessed=2 * (2 * queries.size + mine.size + mates.size),
            transcendentals=queries.size // (mine.shape[1] // 2) * (mine.shape[0] + mates.shape[0]),
        ),
        compiler_params=pltpu.CompilerParams(vmem_limit_bytes=24 * 2**20),
        name="attention",
    )(place, queries, mine, mates)


def swap_dp(array):
    return lax.ppermute(array, "dp", SWAP)


def swap_core(array):
    return lax.ppermute(array, "core", SWAP)


FLIP_Y, RIGHT, LEFT, ACROSS = (1, 0), (0, 1), (0, 3), (0, 2)


def hop(array, even=None, odd=None):
    pairs = []
    for core, step in enumerate((even, odd)):
        if step is not None:
            for y in range(2):
                for x in range(4):
                    target = (y ^ step[0]) * 4 + (x + step[1]) % 4
                    pairs.append(((y * 4 + x) * 2 + core, target * 2 + core))
    return lax.ppermute(array, ("yh", "x", "core"), pairs)


def halves(array, part):
    size = array.shape[-1] // 2
    own = lax.dynamic_slice_in_dim(array, part * size, size, array.ndim - 1)
    other = lax.dynamic_slice_in_dim(array, (1 - part) * size, size, array.ndim - 1)
    return own, other


def ring_sum_exp(terms):
    count = 8
    terms = terms.reshape(terms.shape[0], count, -1, terms.shape[-1])

    def own(offset):
        return terms[:, offset % count]

    up_pairs = [(i, (i + 1) % count) for i in range(count)]
    down_pairs = [(i, (i + count - 1) % count) for i in range(count)]
    up, down = own(4), own(-3)
    for step in range(4):
        up = lax.ppermute(up, "exp", up_pairs)
        if step < 3:
            up = (up.astype(F32) + own(3 - step).astype(F32)).astype(BF16)
            down = lax.ppermute(down, "exp", down_pairs)
            if step < 2:
                down = (down.astype(F32) + own(step - 2).astype(F32)).astype(BF16)
    return (up.astype(F32) + down.astype(F32) + own(0).astype(F32)).astype(BF16)


def on_device(
    tokens, norm_in, w_qkv, w_out, norm_mid, w_router, w_gate_up, w_down, expert_ids, slot_index
):
    part = lax.axis_index("dp")
    core = lax.axis_index("core")
    chip = lax.axis_index("yh") * 4 + lax.axis_index("x")
    tok_rows = tokens.shape[1]
    width = tokens.shape[2]
    half = width // 2
    head_dim = w_qkv.shape[3]

    tokens_own, tokens_other = halves(tokens[0], part)
    tokens_peer = swap_dp(tokens_other)
    wide = tokens[0].astype(F32)
    scale_in = lax.rsqrt(jnp.mean(wide * wide, axis=-1) + EPSILON)
    scale_peer = swap_dp(scale_in[None])[0]
    gain_own = halves(norm_in, part)[0].astype(F32)
    normed_own = (tokens_own.astype(F32) * scale_in[:, None] * gain_own).astype(BF16)
    normed_peer = (tokens_peer.astype(F32) * scale_peer[:, None] * gain_own).astype(BF16)
    weights_in = w_qkv.reshape(half, -1)
    to_peer = jnp.dot(normed_peer, weights_in, preferred_element_type=F32).astype(BF16)
    from_peer = swap_dp(to_peer)
    projected_own = jnp.dot(normed_own, weights_in, preferred_element_type=F32)

    gate_up_part, _ = lax.optimization_barrier((w_gate_up[0], (tokens_other, scale_in)))
    gate_up_full = lax.all_gather(gate_up_part, "dp", axis=0, tiled=True)

    query_idx = (chip * 2 + core) * tok_rows + jnp.arange(tok_rows, dtype=jnp.int32)
    angles = rope_angles(query_idx.astype(F32), head_dim)
    cosine, sine = jnp.cos(angles), jnp.sin(angles)
    queries, keys_values = rotary(
        projected_own,
        from_peer,
        jnp.concatenate([cosine, cosine], axis=1),
        jnp.concatenate([-sine, sine], axis=1),
    )

    pair = jnp.concatenate([keys_values, swap_core(keys_values)])
    pieces = []
    for step in range(1, 5):
        pairs = [(i * 2, (i + step) * 2) for i in range(8 - step)]
        pairs += [(i * 2 + 1, (i + step + 4) * 2 + 1) for i in range(4 - step)]
        pieces.append(lax.ppermute(pair, CHIPS + ("core",), pairs))
    earlier = jnp.concatenate(pieces)
    mates = swap_core(earlier)
    attended = attention(
        jnp.stack([chip, core]), queries, jnp.concatenate([pair, earlier]), mates
    )

    rows = tok_rows // 8
    attended = lax.dynamic_slice_in_dim(
        jnp.concatenate([attended, attended]), lax.axis_index("exp") * rows, tok_rows, 0
    )

    both = jnp.stack([attended, swap_dp(attended)])
    partial_sum = jnp.einsum(
        "bth,hd->btd", both, w_out.reshape(-1, half), preferred_element_type=F32
    ).astype(BF16)
    summed = ring_sum_exp(partial_sum)
    summed, down_mate = lax.optimization_barrier((summed, swap_core(w_down[0])))
    head_total = jnp.concatenate([summed[0], swap_dp(summed[1])], axis=-1)
    head_total = jnp.concatenate(halves(head_total, part), axis=-1).astype(F32)
    own_tokens = lax.dynamic_slice_in_dim(tokens[0], lax.axis_index("exp") * rows, rows, 0)
    mixed = (own_tokens.astype(F32) + head_total).astype(BF16)

    wide_mid = mixed.astype(F32)
    scale_mid = lax.rsqrt(jnp.mean(wide_mid * wide_mid, axis=-1, keepdims=True) + EPSILON)
    normed_mid = (wide_mid * scale_mid * norm_mid.astype(F32)).astype(BF16)
    logits = jnp.dot(normed_mid, w_router, preferred_element_type=F32)
    expert_count = w_router.shape[1]
    choice_ids = expert_ids[0]
    picks = choice_ids[:, :, None] == jnp.arange(expert_count, dtype=jnp.int32)[None, None, :]
    chosen = jnp.sum(jnp.where(picks, logits[:, None, :], 0.0), axis=-1)
    gate_first = 1.0 / (1.0 + jnp.exp(chosen[:, 1] - chosen[:, 0]))
    gate_second = 1.0 - gate_first
    capacity = 6
    flat_index = choice_ids * capacity + slot_index[0]
    slot_cols = jnp.arange(expert_count * capacity, dtype=jnp.int32)
    combiner = gate_first[:, None] * (flat_index[:, 0:1] == slot_cols[None, :]).astype(
        F32
    ) + gate_second[:, None] * (flat_index[:, 1:2] == slot_cols[None, :]).astype(F32)
    combiners = jnp.stack([combiner, swap_dp(combiner)])
    placer = jnp.logical_or(
        slot_cols[:, None] == flat_index[None, :, 0], slot_cols[:, None] == flat_index[None, :, 1]
    ).astype(BF16)
    buffer_rows = jnp.dot(placer, normed_mid, preferred_element_type=F32).astype(BF16)
    buffer_rows = buffer_rows.reshape(expert_count, capacity, width)
    received = lax.all_to_all(buffer_rows, "exp", split_axis=0, concat_axis=0, tiled=True)
    received = received.reshape(expert_count * capacity, width)

    first = core == 0
    from_1 = hop(received, even=FLIP_Y, odd=RIGHT)
    from_2 = hop(received, odd=LEFT)
    from_3 = hop(received, odd=ACROSS)
    near = jnp.concatenate([received, from_1])
    side = jnp.concatenate([from_2, from_3])
    near, side, gate_up_full = lax.optimization_barrier((near, side, gate_up_full))
    gate_up_mate = swap_core(gate_up_full)
    mixed_rows = jnp.where(first, near, side)
    near, side, mixed_rows = lax.optimization_barrier((near, side, mixed_rows))
    far_1 = hop(near, even=RIGHT, odd=FLIP_Y)
    far_2 = hop(mixed_rows, even=LEFT, odd=FLIP_Y)
    far_3 = hop(near, even=ACROSS)
    expert_rows = jnp.concatenate([near, far_1, far_2, jnp.where(first, far_3, side)])
    down = 0.0
    for weights, down_part in ((gate_up_full, w_down[0]), (gate_up_mate, down_mate)):
        gate_up = jnp.einsum("rd,djf->rjf", expert_rows, weights, preferred_element_type=F32)
        hidden = (jax.nn.silu(gate_up[:, 0]) * gate_up[:, 1]).astype(BF16)
        hidden = jnp.stack([hidden, swap_dp(hidden)])
        down = down + jnp.einsum("prf,fd->prd", hidden, down_part, preferred_element_type=F32)
    down = down.astype(BF16)

    slots = expert_count * capacity
    res_near, res_1, res_2, res_3 = (
        down[:, i * 2 * slots : (i + 1) * 2 * slots] for i in range(4)
    )
    back_1 = hop(res_1, even=LEFT, odd=FLIP_Y).astype(F32)
    back_2 = hop(res_2, even=RIGHT, odd=FLIP_Y).astype(F32)
    back_3 = hop(res_3, even=ACROSS).astype(F32)
    sum_near = res_near.astype(F32) + back_1 + jnp.where(first, back_2, 0.0) + back_3
    sum_side = (res_3.astype(F32) + back_2).astype(BF16)
    total = (
        sum_near[:, :slots]
        + hop(sum_near[:, slots:].astype(BF16), even=FLIP_Y, odd=LEFT).astype(F32)
        + hop(sum_side[:, :slots], odd=RIGHT).astype(F32)
        + hop(sum_side[:, slots:], odd=ACROSS).astype(F32)
    )
    expert_out = total.astype(BF16).reshape(2, expert_count, capacity, half)
    returned = lax.all_to_all(expert_out, "exp", split_axis=1, concat_axis=1, tiled=True)
    returned = returned.reshape(2, expert_count * capacity, half)
    moe_both = jnp.einsum(
        "prc,pcd->prd", combiners, returned.astype(F32), precision=lax.Precision.HIGHEST
    )
    moe_total = jnp.concatenate(
        [moe_both[0], swap_dp(moe_both[1].astype(BF16)).astype(F32)], axis=-1
    )
    moe_total = jnp.concatenate(halves(moe_total, part), axis=-1)
    return (mixed.astype(F32) + moe_total).astype(BF16)[None]


def solution(mesh):
    fine = Mesh(mesh.devices.reshape(2, 4, 2, 8, 2), ("yh", "x", "core", "exp", "dp"))
    ctx = ("yh", "x", "core")
    rows = ctx + ("exp",)
    placed = (
        P("dp", ctx, None),
        P(),
        P("dp", "exp", None, None),
        P("exp", None, None, "dp"),
        P(),
        P(),
        P("exp", "dp", None, ctx),
        P("exp", ctx, "dp"),
        P("dp", rows, None),
        P("dp", rows, None),
    )
    return jax.shard_map(
        on_device,
        mesh=fine,
        in_specs=placed,
        out_specs=P("dp", rows, None),
        check_vma=False,
    )
```
